768 devices in a mesh: band: 192 (over z, y, core), lon: 4 (over x).
Axes of the slice: x: 4, y: 8, z: 12, core: 2. Of those that a mesh axis runs over, the one named last changes fastest.
Arguments:
- thermal_state: bfloat16 [768, 8, 5136], P('band', None, 'lon'), may hold values from -6 to 6
- moisture_ratio: bfloat16 [768, 8, 5136], P('band', None, 'lon'), may hold values from 0 to 1
- ground_height_energy: bfloat16 [768, 5136], P('band', 'lon'), may hold values from -6 to 6
- column_summing_operator: float32 [8, 8], replicated, may hold values from -2 to 2
- polynomial_table: bfloat16 [768, 4, 192, 768], P('band', 'lon'), may hold values from -12 to 12
- parallel_angle_kept: int32 [768], P('band'), may hold values from 0 to 767, each once
- zonal_order_for_entry: int32 [768], P('band'), may hold values from 0 to 767, each once
- layer_for_entry: int32 [8], replicated, may hold values from 0 to 7, each once
Outputs:
- spectral: float32 [768, 2, 8, 768], P('band', None, 'lon')
The draws below stay inside these ranges and needn't reach their ends.
Inputs may be any that keep to these rules, and one draw needn't show every extreme that they name: `parallel_angle_kept`: each latitude of the window is the latitude of exactly one stored row. `zonal_order_for_entry`: each zonal wavenumber is held in exactly one slot. `layer_for_entry`: each level is held in exactly one slot.
All inputs are finite; a program needn't handle non-finite values.
Results may differ from the reference program's by a relative error of at most 0.0049.
Values may be sent and summed in bfloat16 or wider, within the bound.
A program may use at most 64 MiB of HBM per device.

```python
import math
import jax
import jax.numpy as jnp
from jax import lax

SIGMA_LAYERS = 8
WIDEST_CIRCLE = 5136
BANDS = 192
ROW_BAND = 4
PARALLEL_COUNT = 768
WAVES = 768


def levels(stream_key, extent, split, smallest, largest):
    loudness = 1.0
    for position, parts in split:
        heights = jax.random.uniform(jax.random.fold_in(jax.random.fold_in(stream_key, 6), position), (parts,), jnp.float32, smallest / len(split), largest / len(split))
        loudness = loudness * jnp.repeat(jnp.exp(heights), extent[position] // parts).reshape((-1,) + (1,) * (len(extent) - 1 - position))
    return loudness


def bell_draw(stream_key, extent, scale, limit, split=(), kind=jnp.bfloat16):
    factor_of = levels(stream_key, extent, split, -0.22, 0.18) if split else 1.0
    array = jax.random.normal(stream_key, extent, jnp.float32) * scale * factor_of
    return jnp.minimum(jnp.maximum(array, -limit), limit).astype(kind)


def setup_inputs(seed: int = 0) -> dict:
    key_of = jax.random.split(jax.random.key(seed), 9)
    thermal_state = bell_draw(key_of[0], (PARALLEL_COUNT, SIGMA_LAYERS, WIDEST_CIRCLE), 1.0, 6.0, ((0, 192), (2, 4)))
    moisture_ratio = jnp.clip(1.0 * jax.random.uniform(key_of[1], (PARALLEL_COUNT, SIGMA_LAYERS, WIDEST_CIRCLE), jnp.float32) ** levels(key_of[1], (PARALLEL_COUNT, SIGMA_LAYERS, WIDEST_CIRCLE), ((0, 192), (2, 4)), -0.2, 0.2), 0.0, 1.0).astype(jnp.bfloat16)
    ground_height_energy = bell_draw(key_of[2], (PARALLEL_COUNT, WIDEST_CIRCLE), 1.0, 6.0, ((0, 192), (1, 4)))
    column_summing_operator = bell_draw(key_of[3], (SIGMA_LAYERS, SIGMA_LAYERS), SIGMA_LAYERS ** -0.5, 2.0, (), jnp.float32)
    polynomial_table = bell_draw(key_of[4], (WAVES, ROW_BAND, BANDS, WAVES), 2.0, 12.0, ((0, 192), (1, 4)))
    parallel_angle_kept = jax.random.permutation(key_of[5], PARALLEL_COUNT).astype(jnp.int32)
    zonal_order_for_entry = jax.random.permutation(key_of[6], WAVES).astype(jnp.int32)
    layer_for_entry = jax.random.permutation(key_of[7], SIGMA_LAYERS).astype(jnp.int32)
    return dict(thermal_state=thermal_state, moisture_ratio=moisture_ratio, ground_height_energy=ground_height_energy, column_summing_operator=column_summing_operator, polynomial_table=polynomial_table, parallel_angle_kept=parallel_angle_kept, zonal_order_for_entry=zonal_order_for_entry, layer_for_entry=layer_for_entry)


def fourier_row(grid_row, length, wave_count):
    points = lax.iota(jnp.int32, grid_row.shape[1])
    wave_ids = lax.iota(jnp.int32, wave_count)
    residue = (points[:, None] * wave_ids[None, :]) % length
    angles = residue.astype(jnp.float32) * (2.0 * math.pi / length.astype(jnp.float32))
    inside = (points < length)[:, None]
    inverse = 1.0 / length.astype(jnp.float32)
    cos_table = jnp.where(inside, jnp.cos(angles) * inverse, 0.0).astype(jnp.bfloat16)
    sin_table = jnp.where(inside, -jnp.sin(angles) * inverse, 0.0).astype(jnp.bfloat16)
    tables = jnp.concatenate([cos_table, sin_table], axis=1)
    return jnp.dot(grid_row, tables, preferred_element_type=jnp.float32).astype(jnp.bfloat16)


def reference(thermal_state, moisture_ratio, ground_height_energy, column_summing_operator, polynomial_table, parallel_angle_kept, zonal_order_for_entry, layer_for_entry):
    density_thermal_state = thermal_state.astype(jnp.float32) * (1.0 + 0.608 * moisture_ratio.astype(jnp.float32))
    geopotential = ground_height_energy.astype(jnp.float32)[:, None, :] + jnp.einsum(
        "gv,wvh->wgh", column_summing_operator, density_thermal_state, precision=lax.Precision.HIGHEST)
    geopotential = geopotential.astype(jnp.bfloat16)

    def one_row(inputs):
        grid_row, latitude = inputs
        distance = jnp.minimum(latitude, PARALLEL_COUNT - 1 - latitude)
        length = (WIDEST_CIRCLE - 4 * (PARALLEL_COUNT // 2 - 1 - distance)).astype(jnp.int32)
        return fourier_row(grid_row, length, WAVES)

    fourier = lax.map(one_row, (geopotential, parallel_angle_kept))
    cos_part = fourier[:, :, :WAVES]
    sin_part = fourier[:, :, WAVES:]

    def one_slot(inputs):
        slot_weights, wavenumber = inputs
        quadrature_weights = jnp.transpose(slot_weights, (1, 0, 2)).reshape(PARALLEL_COUNT, WAVES).astype(jnp.float32)
        cos_column = lax.dynamic_index_in_dim(cos_part, wavenumber, 2, keepdims=False).astype(jnp.float32)
        sin_column = lax.dynamic_index_in_dim(sin_part, wavenumber, 2, keepdims=False).astype(jnp.float32)
        stacked_fields = jnp.stack([cos_column, sin_column])
        transform_output = jnp.einsum("asv,sm->avm", stacked_fields, quadrature_weights, precision=lax.Precision.HIGHEST)
        keep_mask = (jnp.arange(WAVES, dtype=jnp.int32) < (WAVES - wavenumber)).astype(jnp.float32)
        return transform_output * keep_mask

    spectral_raw = lax.map(one_slot, (polynomial_table, zonal_order_for_entry))
    return jnp.take(spectral_raw, layer_for_entry, axis=2)
```

```python
import jax
import jax.numpy as jnp
from jax import lax
from jax.experimental import pallas as pl
from jax.experimental.pallas import tpu as pltpu
from jax.sharding import PartitionSpec as P

Z, Y, CORES, LON = 12, 8, 2, 4
YC = Y * CORES
BANDS = Z * YC
LEVELS = 8
WAVES = 768
WIDEST = 5136
PIECE = WIDEST // LON
HALF = 768
BLOCK = 256
BLOCKS = LON * 2 * (HALF // BLOCK)
F32, BF16, I32 = jnp.float32, jnp.bfloat16, jnp.int32
MESH = pl.DeviceIdType.MESH

COS = (1.0, -4.93480110168457, 4.058692932128906, -1.335150122642517, 0.2350122481584549, -0.025341978296637535, 0.0015877870609983802)
SIN = (3.1415927410125732, -5.167712688446045, 2.5501599311828613, -0.5992405414581299, 0.08207812905311584, -0.007271677255630493, 0.000393970258301124)


def iota(shape, dim):
    return lax.broadcasted_iota(I32, shape, dim)


def circle(product, length, inverse):
    residue = product - jnp.round(product * inverse) * length
    x = residue * (inverse * 2.0)
    y = x * x
    c = COS[-1]
    s = SIN[-1]
    for a, b in zip(COS[-2::-1], SIN[-2::-1]):
        c = c * y + a
        s = s * y + b
    return c, s * x


def row_length(latitude):
    distance = jnp.minimum(latitude, LON * BANDS - 1 - latitude)
    return WIDEST - 4 * (LON * BANDS // 2 - 1 - distance)


def permuted_operator(operator, layers):
    t = iota((LEVELS, 1), 0)
    level = jnp.zeros((LEVELS, 1), I32)
    for i in range(LEVELS):
        level = jnp.where(t == i, layers[i], level)
    out = jnp.zeros((LEVELS, LEVELS), F32)
    for i in range(LEVELS):
        out = jnp.where(level == i, operator[i : i + 1, :], out)
    return out


def vertical_sum(temperature, moisture, ground, operator):
    virtual = temperature.astype(F32) * (1.0 + 0.608 * moisture.astype(F32))
    total = operator[:, 0:1] * virtual[0:1, :]
    for j in range(1, LEVELS):
        total = total + operator[:, j : j + 1] * virtual[j : j + 1, :]
    return total + ground.astype(F32)


def pack_piece(low, high, lon, length):
    both = jnp.concatenate([low, high], axis=0)
    point = lon * PIECE + jnp.where(iota((16, HALF), 0) >= 8, HALF, 0) + iota((16, HALF), 1)
    return jnp.where(point < length, both, 0.0).astype(BF16)


def phase_points():
    a = iota((BLOCKS, 128), 0)
    return ((a >> 3) * BLOCK + ((a >> 1) & 3) * PIECE + (a & 1) * HALF).astype(F32)


def legendre_row_of(row):
    return (row >> 2) & 3


def coefficient_order():
    r = iota((128, 128), 0)
    level = r & 7
    lane = (r & 64) + (level >> 1) * 16 + ((r >> 4) & 3) * 4 + ((r >> 3) & 1) * 2 + (level & 1)
    return jnp.where(lane == iota((128, 128), 1), 1.0, 0.0).astype(BF16)


def by_target():
    i = iota((128, 96), 0)
    source = (2 * (i & 7) + (i >> 6)) * Y + ((i >> 3) & 7)
    return jnp.where(source == iota((128, 96), 1), 1.0, 0.0).astype(BF16)


def by_band():
    i = iota((256, BANDS), 0)
    band = (2 * (i & 7) + (i >> 7)) * YC + ((i >> 3) & 15)
    return jnp.where(band == iota((256, BANDS), 1), 1.0, 0.0).astype(BF16)


def split_cores(rows):
    even, odd = rows[:64], rows[64:]
    first = iota((64, 128), 1) < 64
    return (
        jnp.where(first, even, pltpu.roll(odd, 64, 1)),
        jnp.where(first, pltpu.roll(even, 64, 1), odd),
    )


def dot(a, b):
    return jnp.dot(a, b, preferred_element_type=F32)


def kernel(
    latitudes, orders, layers, temperature, moisture, ground, operator, polynomial,
    out,
    t_in, q_in, g_in, o_in, p_in, fields, piece_out, piece_in, order_1, order_2, order_rows,
    tables, phases, columns, send_1, recv_1, send_2, recv_2, part_out, part_in,
    load_sem, send_sem, recv_sem,
):
    band, lon = lax.axis_index("band"), lax.axis_index("lon")
    z, yc = band // YC, band % YC
    y, core = yc // CORES, yc % CORES

    def over_z(o):
        return lax.rem(z + o, Z)

    def over_yc(o):
        return lax.rem(yc + o, YC)

    def over_lon(o):
        return lax.rem(lon + o, LON)

    barrier = pltpu.get_barrier_semaphore()
    for o in range(1, LON):
        pl.semaphore_signal(barrier, 1, device_id={"lon": over_lon(o)}, device_id_type=MESH)
    for o in range(1, YC):
        pl.semaphore_signal(barrier, 1, device_id={"band": z * YC + over_yc(o)}, device_id_type=MESH)
    for o in range(1, Z):
        pl.semaphore_signal(barrier, 1, device_id={"band": over_z(o) * YC + yc}, device_id_type=MESH)

    loads = [
        pltpu.make_async_copy(source, target, load_sem.at[i])
        for i, (source, target) in enumerate(
            ((temperature, t_in), (moisture, q_in), (ground, g_in), (operator, o_in), (polynomial.at[:, 0], p_in))
        )
    ]
    for load in loads:
        load.start()

    def exchange(stage, count, partner, source, target):
        for o in range(1, count):
            pltpu.make_async_remote_copy(
                src_ref=source(o), dst_ref=target, send_sem=send_sem.at[stage], recv_sem=recv_sem.at[stage],
                device_id=partner(o), device_id_type=MESH,
            ).start()

    def wait_recv(stage, ref):
        pltpu.make_async_copy(ref, ref, recv_sem.at[stage]).wait()

    def wait_send(stage, ref):
        pltpu.make_async_copy(ref, ref, send_sem.at[stage]).wait()

    def to_yc(o):
        return {"band": z * YC + over_yc(o)}

    def to_z(o):
        return {"band": over_z(o) * YC + yc}

    def to_lon(o):
        return {"lon": over_lon(o)}

    own_row, own_lane = iota((8, 128), 0) == y, iota((8, 128), 1) - core * 4
    tile = jnp.zeros((8, 128), F32)
    for s in range(4):
        tile = jnp.where(own_row & (own_lane == s), orders[s].astype(F32), tile)
    order_1[yc] = tile
    fields[:, :, 1280:] = jnp.zeros((4, LEVELS, 2 * HALF - 1280), F32)
    pl.semaphore_wait(barrier, LON + YC + Z - 3)
    exchange(0, YC, to_yc, lambda o: order_1.at[yc], order_1.at[yc])

    for load in loads[:4]:
        load.wait()
    operator_rows = permuted_operator(o_in[...], [layers[i] for i in range(LEVELS)])
    for r in range(4):
        fields[r, :, :PIECE] = vertical_sum(t_in[r], q_in[r], g_in[r : r + 1], operator_rows)
        piece_out[r] = pack_piece(fields[r, :, :HALF], fields[r, :, HALF:], lon, row_length(latitudes[r]))
    exchange(1, LON, to_lon, lambda o: piece_out.at[over_lon(o)], piece_in.at[lon])
    piece_in[lon] = piece_out[lon]

    wait_recv(0, order_1.at[pl.ds(0, YC - 1)])
    order_2[z] = jnp.sum(order_1[...], axis=0)
    order_2[pl.ds(Z, 4)] = jnp.zeros((4, 8, 128), F32)
    exchange(2, Z, to_z, lambda o: order_2.at[z], order_2.at[z])
    wait_recv(2, order_2.at[pl.ds(0, Z - 1)])
    order_rows[...] = order_2[...].reshape(128, 128).T[:8]

    length = jnp.full((1, 128), row_length(latitudes[lon]), I32).astype(F32)
    inverse = 1.0 / length

    def table(n, carry):
        m = order_rows[pl.ds(n, 1), :]
        step = iota((16, 128), 0).astype(F32)
        c0, s0 = circle(step * m, length, inverse)
        c1, s1 = circle(step * 16.0 * m, length, inverse)
        for b in range(16):
            c, s = c1[b : b + 1], s1[b : b + 1]
            tables[n, b * 16 : b * 16 + 16, :128] = (c * c0 - s * s0).astype(BF16)
            tables[n, b * 16 : b * 16 + 16, 128:] = (s * c0 + c * s0).astype(BF16)
        c, s = circle(phase_points() * m, length, inverse)
        phases[n, :, :128] = c * inverse
        phases[n, :, 128:] = s * inverse
        return carry

    lax.fori_loop(0, 8, table, 0)

    wait_recv(1, piece_in.at[pl.ds(0, LON - 1)])

    def transform(n, carry):
        c = jnp.zeros((8, 128), F32)
        s = jnp.zeros((8, 128), F32)
        for j in range(HALF // BLOCK):
            block = piece_in[:, :, j * BLOCK : (j + 1) * BLOCK].reshape(LON * 16, BLOCK)
            sums = dot(block, tables[n])
            for i in range(8):
                a = j * 8 + i
                pc, ps = phases[n, a : a + 1, :128], phases[n, a : a + 1, 128:]
                gc, gs = sums[i * 8 : i * 8 + 8, :128], sums[i * 8 : i * 8 + 8, 128:]
                c = c + (pc * gc - ps * gs)
                s = s - (ps * gc + pc * gs)
        columns[2 * n] = c
        columns[2 * n + 1] = s
        return carry

    lax.fori_loop(0, 8, transform, 0)

    turned = columns[...].reshape(128, 128).T.astype(BF16)
    send_1[...] = dot(turned, coefficient_order()).reshape(16, 8, 128)
    exchange(3, Z, to_z, lambda o: send_1.at[over_z(o)], recv_1.at[z])
    recv_1[z] = send_1[z]
    wait_recv(3, recv_1.at[pl.ds(0, Z - 1)])

    first, second = split_cores(dot(by_target(), recv_1[...].reshape(96, 128).astype(BF16)))
    for i in range(Y):
        send_2[2 * i] = first[i * 8 : i * 8 + 8]
        send_2[2 * i + 1] = second[i * 8 : i * 8 + 8]
    exchange(4, YC, to_yc, lambda o: send_2.at[over_yc(o)], recv_2.at[yc])
    recv_2[yc] = send_2[yc]
    loads[4].wait()
    wait_recv(4, recv_2.at[pl.ds(0, YC - 1)])

    turned = recv_2[...].reshape(128, 128).T.astype(BF16)
    rows = dot(jnp.concatenate([turned[:64], turned[64:]], axis=1), by_band())
    slot = legendre_row_of(iota((64, BANDS), 0))
    total = jnp.zeros((64, WAVES), F32)
    for s in range(4):
        total = total + dot(jnp.where(slot == s, rows, 0.0).astype(BF16), p_in[s])
    part_out[...] = total.reshape(LON, 16, WAVES)
    exchange(5, LON, to_lon, lambda o: part_out.at[over_lon(o)], part_in.at[lon])
    part_in[lon] = part_out[lon]
    wait_recv(5, part_in.at[pl.ds(0, LON - 1)])

    slot = legendre_row_of(iota((16, 1), 0))
    limit = jnp.zeros((16, 1), I32)
    for s in range(4):
        limit = jnp.where(slot == s, WAVES - orders[s], limit)
    summed = (part_in[0] + part_in[1]) + (part_in[2] + part_in[3])
    out[...] = jnp.where(iota((16, WAVES), 1) < limit, summed, 0.0)

    wait_send(0, order_1.at[pl.ds(0, YC - 1)])
    wait_send(1, piece_out.at[pl.ds(0, LON - 1)])
    wait_send(2, order_2.at[pl.ds(0, Z - 1)])
    wait_send(3, send_1.at[pl.ds(0, Z - 1)])
    wait_send(4, send_2.at[pl.ds(0, YC - 1)])
    wait_send(5, part_out.at[pl.ds(0, LON - 1)])


def body(temperature, moisture, ground, operator, polynomial, latitudes, orders, layers):
    anywhere = pl.BlockSpec(memory_space=pl.ANY)
    scalars = pl.BlockSpec(memory_space=pltpu.SMEM)
    vmem = pltpu.VMEM
    flat = pl.pallas_call(
        kernel,
        out_shape=jax.ShapeDtypeStruct((16, WAVES), F32),
        in_specs=[scalars] * 3 + [anywhere] * 5,
        out_specs=pl.BlockSpec(memory_space=pltpu.VMEM),
        scratch_shapes=[
            vmem(temperature.shape, BF16),
            vmem(moisture.shape, BF16),
            vmem(ground.shape, BF16),
            vmem(operator.shape, F32),
            vmem((4, BANDS, WAVES), BF16),
            vmem((4, LEVELS, 2 * HALF), F32),
            vmem((LON, 16, HALF), BF16),
            vmem((LON, 16, HALF), BF16),
            vmem((YC, 8, 128), F32),
            vmem((16, 8, 128), F32),
            vmem((8, 128), F32),
            vmem((8, BLOCK, 256), BF16),
            vmem((8, BLOCKS, 256), F32),
            vmem((16, 8, 128), F32),
            vmem((16, 8, 128), F32),
            vmem((Z, 8, 128), F32),
            vmem((YC, 8, 128), F32),
            vmem((YC, 8, 128), F32),
            vmem((LON, 16, WAVES), F32),
            vmem((LON, 16, WAVES), F32),
            pltpu.SemaphoreType.DMA((5,)),
            pltpu.SemaphoreType.DMA((6,)),
            pltpu.SemaphoreType.DMA((6,)),
        ],
        compiler_params=pltpu.CompilerParams(
            collective_id=0, has_side_effects=True, vmem_limit_bytes=32 * 1024 * 1024
        ),
    )(latitudes, orders, layers, temperature, moisture, ground, operator, polynomial)
    return flat.reshape(4, 2, 2, WAVES)


def solution(mesh):
    placed = (
        P("band", None, "lon"),
        P("band", None, "lon"),
        P("band", "lon"),
        P(),
        P("band", "lon", None, None),
        P("band"),
        P("band"),
        P(),
    )
    return jax.shard_map(
        body, mesh=mesh, in_specs=placed, out_specs=P("band", None, "lon", None), check_vma=False
    )
```

```python
import jax
import jax.numpy as jnp
from jax import lax
from jax.experimental import pallas as pl
from jax.experimental.pallas import tpu as pltpu
from jax.sharding import PartitionSpec as P

Z, Y, CORES, LON = 12, 8, 2, 4
YC = Y * CORES
BANDS = Z * YC
LEVELS = 8
WAVES = 768
WIDEST = 5136
PIECE = WIDEST // LON
HALF = 768
BLOCK = 256
BLOCKS = LON * 2 * (HALF // BLOCK)
F32, BF16, I32 = jnp.float32, jnp.bfloat16, jnp.int32
MESH = pl.DeviceIdType.MESH

COS = (1.0, -4.93480110168457, 4.058692932128906, -1.335150122642517, 0.2350122481584549, -0.025341978296637535, 0.0015877870609983802)
SIN = (3.1415927410125732, -5.167712688446045, 2.5501599311828613, -0.5992405414581299, 0.08207812905311584, -0.007271677255630493, 0.000393970258301124)


def iota(shape, dim):
    return lax.broadcasted_iota(I32, shape, dim)


def circle(product, length, inverse):
    residue = product - jnp.round(product * inverse) * length
    x = residue * (inverse * 2.0)
    y = x * x
    c = COS[-1]
    s = SIN[-1]
    for a, b in zip(COS[-2::-1], SIN[-2::-1]):
        c = c * y + a
        s = s * y + b
    return c, s * x


def row_length(latitude):
    distance = jnp.minimum(latitude, LON * BANDS - 1 - latitude)
    return WIDEST - 4 * (LON * BANDS // 2 - 1 - distance)


def permuted_operator(operator, layers):
    t = iota((LEVELS, 1), 0)
    level = jnp.zeros((LEVELS, 1), I32)
    for i in range(LEVELS):
        level = jnp.where(t == i, layers[i], level)
    out = jnp.zeros((LEVELS, LEVELS), F32)
    for i in range(LEVELS):
        out = jnp.where(level == i, operator[i : i + 1, :], out)
    return out


def vertical_sum(temperature, moisture, ground, operator):
    virtual = temperature.astype(F32) * (1.0 + 0.608 * moisture.astype(F32))
    total = operator[:, 0:1] * virtual[0:1, :]
    for j in range(1, LEVELS):
        total = total + operator[:, j : j + 1] * virtual[j : j + 1, :]
    return total + ground.astype(F32)


def pack_piece(low, high, lon, length):
    both = jnp.concatenate([low, high], axis=0)
    point = lon * PIECE + jnp.where(iota((16, HALF), 0) >= 8, HALF, 0) + iota((16, HALF), 1)
    return jnp.where(point < length, both, 0.0).astype(BF16)


def phase_points():
    a = iota((BLOCKS, 128), 0)
    return ((a >> 3) * BLOCK + ((a >> 1) & 3) * PIECE + (a & 1) * HALF).astype(F32)


def legendre_row_of(row):
    return (row >> 2) & 3


def coefficient_order():
    r = iota((128, 128), 0)
    level = r & 7
    lane = (r & 64) + (level >> 1) * 16 + ((r >> 4) & 3) * 4 + ((r >> 3) & 1) * 2 + (level & 1)
    return jnp.where(lane == iota((128, 128), 1), 1.0, 0.0).astype(BF16)


def by_target():
    i = iota((128, 96), 0)
    source = (2 * (i & 7) + (i >> 6)) * Y + ((i >> 3) & 7)
    return jnp.where(source == iota((128, 96), 1), 1.0, 0.0).astype(BF16)


def by_band():
    i = iota((256, BANDS), 0)
    band = (2 * (i & 7) + (i >> 7)) * YC + ((i >> 3) & 15)
    return jnp.where(band == iota((256, BANDS), 1), 1.0, 0.0).astype(BF16)


def split_cores(rows):
    even, odd = rows[:64], rows[64:]
    first = iota((64, 128), 1) < 64
    return (
        jnp.where(first, even, pltpu.roll(odd, 64, 1)),
        jnp.where(first, pltpu.roll(even, 64, 1), odd),
    )


def dot(a, b):
    return jnp.dot(a, b, preferred_element_type=F32)


def kernel(
    latitudes, orders, layers, temperature, moisture, ground, operator, polynomial,
    out,
    t_in, q_in, g_in, o_in, p_in, fields, piece_out, piece_in, order_1, order_2, order_rows,
    tables, phases, columns, send_1, recv_1, send_2, recv_2, part_out, part_in,
    load_sem, send_sem, recv_sem,
):
    band, lon = lax.axis_index("band"), lax.axis_index("lon")
    z, yc = band // YC, band % YC
    y, core = yc // CORES, yc % CORES

    def over_z(o):
        return lax.rem(z + o, Z)

    def over_yc(o):
        return lax.rem(yc + o, YC)

    def over_lon(o):
        return lax.rem(lon + o, LON)

    barrier = pltpu.get_barrier_semaphore()
    for o in range(1, LON):
        pl.semaphore_signal(barrier, 1, device_id={"lon": over_lon(o)}, device_id_type=MESH)
    for o in range(1, YC):
        pl.semaphore_signal(barrier, 1, device_id={"band": z * YC + over_yc(o)}, device_id_type=MESH)
    for o in range(1, Z):
        pl.semaphore_signal(barrier, 1, device_id={"band": over_z(o) * YC + yc}, device_id_type=MESH)

    loads = [
        pltpu.make_async_copy(source, target, load_sem.at[i])
        for i, (source, target) in enumerate(
            ((temperature, t_in), (moisture, q_in), (ground, g_in), (operator, o_in), (polynomial.at[:, 0], p_in))
        )
    ]
    for load in loads:
        load.start()

    sent = []

    def exchange(stage, count, partner, source, target, whole):
        sent.append((stage, whole.at[pl.ds(0, count - 1)]))
        for o in range(1, count):
            pltpu.make_async_remote_copy(
                src_ref=source(o), dst_ref=target, send_sem=send_sem.at[stage], recv_sem=recv_sem.at[stage],
                device_id=partner(o), device_id_type=MESH,
            ).start()

    def wait_recv(stage, ref):
        pltpu.make_async_copy(ref, ref, recv_sem.at[stage]).wait()

    def finish():
        for stage, ref in sent:
            pltpu.make_async_copy(ref, ref, send_sem.at[stage]).wait()

    def to_yc(o):
        return {"band": z * YC + over_yc(o)}

    def to_z(o):
        return {"band": over_z(o) * YC + yc}

    def to_lon(o):
        return {"lon": over_lon(o)}

    own_row, own_lane = iota((8, 128), 0) == y, iota((8, 128), 1) - core * 4
    tile = jnp.zeros((8, 128), F32)
    for s in range(4):
        tile = jnp.where(own_row & (own_lane == s), orders[s].astype(F32), tile)
    order_1[yc] = tile
    fields[:, :, 1280:] = jnp.zeros((4, LEVELS, 2 * HALF - 1280), F32)
    pl.semaphore_wait(barrier, LON + YC + Z - 3)
    exchange(0, YC, to_yc, lambda o: order_1.at[yc], order_1.at[yc], order_1)

    for load in loads[:4]:
        load.wait()
    operator_rows = permuted_operator(o_in[...], [layers[i] for i in range(LEVELS)])
    for r in range(4):
        fields[r, :, :PIECE] = vertical_sum(t_in[r], q_in[r], g_in[r : r + 1], operator_rows)
        piece_out[r] = pack_piece(fields[r, :, :HALF], fields[r, :, HALF:], lon, row_length(latitudes[r]))
    exchange(1, LON, to_lon, lambda o: piece_out.at[over_lon(o)], piece_in.at[lon], piece_out)
    piece_in[lon] = piece_out[lon]

    wait_recv(0, order_1.at[pl.ds(0, YC - 1)])
    order_2[z] = jnp.sum(order_1[...], axis=0)
    order_2[pl.ds(Z, 4)] = jnp.zeros((4, 8, 128), F32)
    exchange(2, Z, to_z, lambda o: order_2.at[z], order_2.at[z], order_2)
    wait_recv(2, order_2.at[pl.ds(0, Z - 1)])
    order_rows[...] = order_2[...].reshape(128, 128).T[:8]

    length = jnp.full((1, 128), row_length(latitudes[lon]), I32).astype(F32)
    inverse = 1.0 / length

    def table(n, carry):
        m = order_rows[pl.ds(n, 1), :]
        step = iota((16, 128), 0).astype(F32)
        c0, s0 = circle(step * m, length, inverse)
        c1, s1 = circle(step * 16.0 * m, length, inverse)
        for b in range(16):
            c, s = c1[b : b + 1], s1[b : b + 1]
            tables[n, b * 16 : b * 16 + 16, :128] = (c * c0 - s * s0).astype(BF16)
            tables[n, b * 16 : b * 16 + 16, 128:] = (s * c0 + c * s0).astype(BF16)
        c, s = circle(phase_points() * m, length, inverse)
        phases[n, :, :128] = c * inverse
        phases[n, :, 128:] = s * inverse
        return carry

    lax.fori_loop(0, 8, table, 0)

    wait_recv(1, piece_in.at[pl.ds(0, LON - 1)])

    def transform(n, carry):
        c = jnp.zeros((8, 128), F32)
        s = jnp.zeros((8, 128), F32)
        for j in range(HALF // BLOCK):
            block = piece_in[:, :, j * BLOCK : (j + 1) * BLOCK].reshape(LON * 16, BLOCK)
            sums = dot(block, tables[n])
            for i in range(8):
                a = j * 8 + i
                pc, ps = phases[n, a : a + 1, :128], phases[n, a : a + 1, 128:]
                gc, gs = sums[i * 8 : i * 8 + 8, :128], sums[i * 8 : i * 8 + 8, 128:]
                c = c + (pc * gc - ps * gs)
                s = s - (ps * gc + pc * gs)
        columns[2 * n] = c
        columns[2 * n + 1] = s
        return carry

    lax.fori_loop(0, 8, transform, 0)

    turned = columns[...].reshape(128, 128).T.astype(BF16)
    send_1[...] = dot(turned, coefficient_order()).reshape(16, 8, 128)
    exchange(3, Z, to_z, lambda o: send_1.at[over_z(o)], recv_1.at[z], send_1)
    recv_1[z] = send_1[z]
    wait_recv(3, recv_1.at[pl.ds(0, Z - 1)])

    first, second = split_cores(dot(by_target(), recv_1[...].reshape(96, 128).astype(BF16)))
    for i in range(Y):
        send_2[2 * i] = first[i * 8 : i * 8 + 8]
        send_2[2 * i + 1] = second[i * 8 : i * 8 + 8]
    exchange(4, YC, to_yc, lambda o: send_2.at[over_yc(o)], recv_2.at[yc], send_2)
    recv_2[yc] = send_2[yc]
    loads[4].wait()
    wait_recv(4, recv_2.at[pl.ds(0, YC - 1)])

    turned = recv_2[...].reshape(128, 128).T.astype(BF16)
    rows = dot(jnp.concatenate([turned[:64], turned[64:]], axis=1), by_band())
    slot = legendre_row_of(iota((64, BANDS), 0))
    total = jnp.zeros((64, WAVES), F32)
    for s in range(4):
        total = total + dot(jnp.where(slot == s, rows, 0.0).astype(BF16), p_in[s])
    part_out[...] = total.reshape(LON, 16, WAVES)
    exchange(5, LON, to_lon, lambda o: part_out.at[over_lon(o)], part_in.at[lon], part_out)
    part_in[lon] = part_out[lon]
    wait_recv(5, part_in.at[pl.ds(0, LON - 1)])

    slot = legendre_row_of(iota((16, 1), 0))
    limit = jnp.zeros((16, 1), I32)
    for s in range(4):
        limit = jnp.where(slot == s, WAVES - orders[s], limit)
    summed = (part_in[0] + part_in[1]) + (part_in[2] + part_in[3])
    out[...] = jnp.where(iota((16, WAVES), 1) < limit, summed, 0.0)

    finish()


def body(temperature, moisture, ground, operator, polynomial, latitudes, orders, layers):
    anywhere = pl.BlockSpec(memory_space=pl.ANY)
    scalars = pl.BlockSpec(memory_space=pltpu.SMEM)
    vmem = pltpu.VMEM
    flat = pl.pallas_call(
        kernel,
        out_shape=jax.ShapeDtypeStruct((16, WAVES), F32),
        in_specs=[scalars] * 3 + [anywhere] * 5,
        out_specs=pl.BlockSpec(memory_space=pltpu.VMEM),
        scratch_shapes=[
            vmem(temperature.shape, BF16),
            vmem(moisture.shape, BF16),
            vmem(ground.shape, BF16),
            vmem(operator.shape, F32),
            vmem((4, BANDS, WAVES), BF16),
            vmem((4, LEVELS, 2 * HALF), F32),
            vmem((LON, 16, HALF), BF16),
            vmem((LON, 16, HALF), BF16),
            vmem((YC, 8, 128), F32),
            vmem((16, 8, 128), F32),
            vmem((8, 128), F32),
            vmem((8, BLOCK, 256), BF16),
            vmem((8, BLOCKS, 256), F32),
            vmem((16, 8, 128), F32),
            vmem((16, 8, 128), F32),
            vmem((Z, 8, 128), F32),
            vmem((YC, 8, 128), F32),
            vmem((YC, 8, 128), F32),
            vmem((LON, 16, WAVES), F32),
            vmem((LON, 16, WAVES), F32),
            pltpu.SemaphoreType.DMA((5,)),
            pltpu.SemaphoreType.DMA((6,)),
            pltpu.SemaphoreType.DMA((6,)),
        ],
        compiler_params=pltpu.CompilerParams(
            collective_id=0, has_side_effects=True, vmem_limit_bytes=60 * 1024 * 1024
        ),
    )(latitudes, orders, layers, temperature, moisture, ground, operator, polynomial)
    return flat.reshape(4, 2, 2, WAVES)


def solution(mesh):
    placed = (
        P("band", None, "lon"),
        P("band", None, "lon"),
        P("band", "lon"),
        P(),
        P("band", "lon", None, None),
        P("band"),
        P("band"),
        P(),
    )
    return jax.shard_map(
        body, mesh=mesh, in_specs=placed, out_specs=P("band", None, "lon", None), check_vma=False
    )
```

```python
import jax
import jax.numpy as jnp
from jax import lax
from jax.experimental import pallas as pl
from jax.experimental.pallas import tpu as pltpu
from jax.sharding import PartitionSpec as P

Z, Y, CORES, LON = 12, 8, 2, 4
YC = Y * CORES
BANDS = Z * YC
LEVELS = 8
WAVES = 768
WIDEST = 5136
PIECE = WIDEST // LON
HALF = 768
BLOCK = 256
BLOCKS = LON * 2 * (HALF // BLOCK)
F32, BF16, I32 = jnp.float32, jnp.bfloat16, jnp.int32
MESH = pl.DeviceIdType.MESH

COS = (1.0, -4.93480110168457, 4.058692932128906, -1.335150122642517, 0.2350122481584549, -0.025341978296637535, 0.0015877870609983802)
SIN = (3.1415927410125732, -5.167712688446045, 2.5501599311828613, -0.5992405414581299, 0.08207812905311584, -0.007271677255630493, 0.000393970258301124)


def far_first(count):
    return sorted(range(count), key=lambda o: -min(o, count - o))


def iota(shape, dim):
    return lax.broadcasted_iota(I32, shape, dim)


def circle(product, length, inverse):
    residue = product - jnp.round(product * inverse) * length
    x = residue * (inverse * 2.0)
    y = x * x
    c = COS[-1]
    s = SIN[-1]
    for a, b in zip(COS[-2::-1], SIN[-2::-1]):
        c = c * y + a
        s = s * y + b
    return c, s * x


def row_length(latitude):
    distance = jnp.minimum(latitude, LON * BANDS - 1 - latitude)
    return WIDEST - 4 * (LON * BANDS // 2 - 1 - distance)


def permuted_operator(operator, layers):
    t = iota((LEVELS, 1), 0)
    level = jnp.zeros((LEVELS, 1), I32)
    for i in range(LEVELS):
        level = jnp.where(t == i, layers[i], level)
    out = jnp.zeros((LEVELS, LEVELS), F32)
    for i in range(LEVELS):
        out = jnp.where(level == i, operator[i : i + 1, :], out)
    return out


def vertical_sum(temperature, moisture, ground, operator):
    virtual = temperature.astype(F32) * (1.0 + 0.608 * moisture.astype(F32))
    total = operator[:, 0:1] * virtual[0:1, :]
    for j in range(1, LEVELS):
        total = total + operator[:, j : j + 1] * virtual[j : j + 1, :]
    return total + ground.astype(F32)


def pack_piece(low, high, lon, length):
    both = jnp.concatenate([low, high], axis=0)
    point = lon * PIECE + jnp.where(iota((16, HALF), 0) >= 8, HALF, 0) + iota((16, HALF), 1)
    return jnp.where(point < length, both, 0.0).astype(BF16)


def phase_points():
    a = iota((BLOCKS, 128), 0)
    return ((a >> 3) * BLOCK + ((a >> 1) & 3) * PIECE + (a & 1) * HALF).astype(F32)


def legendre_row_of(row):
    return (row >> 2) & 3


def placement():
    r, column = iota((16, 512), 0), iota((16, 512), 1)
    slot, level = column >> 7, r & 7
    lane = (level >> 1) * 16 + slot * 4 + (r >> 3) * 2 + (level & 1)
    return jnp.where(lane == (column & 127), 1.0, 0.0).astype(BF16)


def dot(a, b):
    return jnp.dot(a, b, preferred_element_type=F32)


def kernel(
    latitudes, orders, layers, temperature, moisture, ground, operator, polynomial,
    out,
    t_in, q_in, g_in, o_in, p_in, fields, piece_out, piece_in, order_1, order_2,
    tables, phases, columns, row_out, row_in, part_out, part_in,
    load_sem, send_sem, recv_sem,
):
    band, lon = lax.axis_index("band"), lax.axis_index("lon")
    z, yc = band // YC, band % YC
    y, core = yc // CORES, yc % CORES

    def over_z(o):
        return lax.rem(z + o, Z)

    def over_yc(o):
        return lax.rem(yc + o, YC)

    def over_lon(o):
        return lax.rem(lon + o, LON)

    barrier = pltpu.get_barrier_semaphore()
    for o in far_first(Z)[:-1]:
        pl.semaphore_signal(barrier, 1, device_id={"band": over_z(o) * YC + yc}, device_id_type=MESH)
    for o in far_first(LON)[:-1]:
        pl.semaphore_signal(barrier, 1, device_id={"lon": over_lon(o)}, device_id_type=MESH)
    for o in far_first(YC)[:-1]:
        pl.semaphore_signal(barrier, 1, device_id={"band": z * YC + over_yc(o)}, device_id_type=MESH)

    loads = [
        pltpu.make_async_copy(source, target, load_sem.at[i])
        for i, (source, target) in enumerate(
            ((temperature, t_in), (moisture, q_in), (ground, g_in), (operator, o_in), (polynomial.at[:, 0], p_in))
        )
    ]
    for load in loads:
        load.start()

    sent = []

    def exchange(stage, count, partner, source, target, whole):
        sent.append((stage, whole.at[pl.ds(0, count - 1)]))
        for o in far_first(count)[:-1]:
            pltpu.make_async_remote_copy(
                src_ref=source(o), dst_ref=target, send_sem=send_sem.at[stage], recv_sem=recv_sem.at[stage],
                device_id=partner(o), device_id_type=MESH,
            ).start()

    def wait_recv(stage, ref):
        pltpu.make_async_copy(ref, ref, recv_sem.at[stage]).wait()

    def finish():
        for stage, ref in sent:
            pltpu.make_async_copy(ref, ref, send_sem.at[stage]).wait()

    def to_yc(o):
        return {"band": z * YC + over_yc(o)}

    def to_z(o):
        return {"band": over_z(o) * YC + yc}

    def to_lon(o):
        return {"lon": over_lon(o)}

    own_row, own_lane = iota((8, 128), 0) == y, iota((8, 128), 1) - core * 4
    tile = jnp.zeros((8, 128), F32)
    for s in range(4):
        tile = jnp.where(own_row & (own_lane == s), orders[s].astype(F32), tile)
    order_1[yc] = tile
    fields[:, :, 1280:] = jnp.zeros((4, LEVELS, 2 * HALF - 1280), F32)
    pl.semaphore_wait(barrier, LON + YC + Z - 3)
    exchange(0, YC, to_yc, lambda o: order_1.at[yc], order_1.at[yc], order_1)

    for load in loads[:4]:
        load.wait()
    operator_rows = permuted_operator(o_in[...], [layers[i] for i in range(LEVELS)])
    for r in range(4):
        fields[r, :, :PIECE] = vertical_sum(t_in[r], q_in[r], g_in[r : r + 1], operator_rows)
        piece_out[r] = pack_piece(fields[r, :, :HALF], fields[r, :, HALF:], lon, row_length(latitudes[r]))
    exchange(1, LON, to_lon, lambda o: piece_out.at[over_lon(o)], piece_in.at[lon], piece_out)
    piece_in[lon] = piece_out[lon]

    wait_recv(0, order_1.at[pl.ds(0, YC - 1)])
    order_2[z] = jnp.sum(order_1[...], axis=0)
    exchange(2, Z, to_z, lambda o: order_2.at[z], order_2.at[z], order_2)

    length = jnp.full((1, 128), row_length(latitudes[lon]), I32).astype(F32)
    inverse = 1.0 / length

    def table(n, carry):
        m = (n * 128 + iota((1, 128), 1)).astype(F32)
        step = iota((16, 128), 0).astype(F32)
        c0, s0 = circle(step * m, length, inverse)
        c1, s1 = circle(step * 16.0 * m, length, inverse)
        for b in range(16):
            c, s = c1[b : b + 1], s1[b : b + 1]
            tables[n, b * 16 : b * 16 + 16, :128] = (c * c0 - s * s0).astype(BF16)
            tables[n, b * 16 : b * 16 + 16, 128:] = (s * c0 + c * s0).astype(BF16)
        c, s = circle(phase_points() * m, length, inverse)
        phases[n, :, :128] = c * inverse
        phases[n, :, 128:] = s * inverse
        return carry

    lax.fori_loop(0, WAVES // 128, table, 0)

    wait_recv(1, piece_in.at[pl.ds(0, LON - 1)])

    def transform(n, carry):
        c = jnp.zeros((8, 128), F32)
        s = jnp.zeros((8, 128), F32)
        for j in range(HALF // BLOCK):
            block = piece_in[:, :, j * BLOCK : (j + 1) * BLOCK].reshape(LON * 16, BLOCK)
            sums = dot(block, tables[n])
            for i in range(8):
                a = j * 8 + i
                pc, ps = phases[n, a : a + 1, :128], phases[n, a : a + 1, 128:]
                gc, gs = sums[i * 8 : i * 8 + 8, :128], sums[i * 8 : i * 8 + 8, 128:]
                c = c + (pc * gc - ps * gs)
                s = s - (ps * gc + pc * gs)
        turned = jnp.concatenate([c, s], axis=0).T.astype(BF16)
        placed = dot(turned, placement()).astype(BF16)
        for s in range(4):
            columns[s, pl.ds(pl.multiple_of(n * 128, 128), 128), :] = placed[:, s * 128 : (s + 1) * 128]
        return carry

    lax.fori_loop(0, WAVES // 128, transform, 0)

    wait_recv(2, order_2.at[pl.ds(0, Z - 1)])
    held = order_2[...].reshape(Z * Y, 128)
    wave = iota((Z * Y, WAVES), 1).astype(F32)
    for c in range(CORES):
        rows = jnp.zeros((Z * Y, 128), F32)
        for s in range(4):
            i = c * 4 + s
            chosen = jnp.where(held[:, i : i + 1] == wave, 1.0, 0.0).astype(BF16)
            rows = rows + dot(chosen, columns[s])
        row_out[c * Z * Y : (c + 1) * Z * Y] = rows.reshape(Z * Y, 1, 128)

    def to_band(target_z, target_y, target_core):
        pltpu.make_async_remote_copy(
            src_ref=row_out.at[target_core * (Z * Y) + target_z * Y + target_y], dst_ref=row_in.at[band],
            send_sem=send_sem.at[3], recv_sem=recv_sem.at[3],
            device_id={"band": (target_z * Y + target_y) * CORES + target_core}, device_id_type=MESH,
        ).start()

    targets = []
    for d in far_first(Y):
        target_y = y + d
        target_y = jnp.where(target_y >= Y, target_y - Y, target_y)
        targets += [(target_y, 1 - core), (target_y, core)]

    def to_other_z(i, carry):
        half = (i + 1) // 2
        target_z = z + Z // 2 + jnp.where(i % 2 == 1, -half, half)
        target_z = jnp.where(target_z >= Z, target_z - Z, target_z)
        for target in targets:
            to_band(target_z, *target)
        return carry

    lax.fori_loop(0, Z - 1, to_other_z, 0)
    for target in targets[:-1]:
        to_band(z, *target)
    sent.append((3, row_out.at[pl.ds(0, BANDS - 1)]))
    row_in[band] = row_out[core * (Z * Y) + z * Y + y]
    loads[4].wait()
    wait_recv(3, row_in.at[pl.ds(0, BANDS - 1)])

    rows = row_in[...].reshape(BANDS, 128).T[:64]
    slot = legendre_row_of(iota((64, BANDS), 0))
    total = jnp.zeros((64, WAVES), F32)
    for s in range(4):
        total = total + dot(jnp.where(slot == s, rows, 0.0).astype(BF16), p_in[s])
    part_out[...] = total.reshape(LON, 16, WAVES).astype(BF16)
    exchange(4, LON, to_lon, lambda o: part_out.at[over_lon(o)], part_in.at[lon], part_out)
    part_in[lon] = part_out[lon]
    wait_recv(4, part_in.at[pl.ds(0, LON - 1)])

    slot = legendre_row_of(iota((16, 1), 0))
    limit = jnp.zeros((16, 1), I32)
    for s in range(4):
        limit = jnp.where(slot == s, WAVES - orders[s], limit)
    part = [part_in[i].astype(F32) for i in range(LON)]
    summed = (part[0] + part[1]) + (part[2] + part[3])
    out[...] = jnp.where(iota((16, WAVES), 1) < limit, summed, 0.0)

    finish()


def body(temperature, moisture, ground, operator, polynomial, latitudes, orders, layers):
    anywhere = pl.BlockSpec(memory_space=pl.ANY)
    scalars = pl.BlockSpec(memory_space=pltpu.SMEM)
    vmem = pltpu.VMEM
    flat = pl.pallas_call(
        kernel,
        out_shape=jax.ShapeDtypeStruct((16, WAVES), F32),
        in_specs=[scalars] * 3 + [anywhere] * 5,
        out_specs=pl.BlockSpec(memory_space=pltpu.VMEM),
        scratch_shapes=[
            vmem(temperature.shape, BF16),
            vmem(moisture.shape, BF16),
            vmem(ground.shape, BF16),
            vmem(operator.shape, F32),
            vmem((4, BANDS, WAVES), BF16),
            vmem((4, LEVELS, 2 * HALF), F32),
            vmem((LON, 16, HALF), BF16),
            vmem((LON, 16, HALF), BF16),
            vmem((YC, 8, 128), F32),
            vmem((Z, 8, 128), F32),
            vmem((WAVES // 128, BLOCK, 256), BF16),
            vmem((WAVES // 128, BLOCKS, 256), F32),
            vmem((4, WAVES, 128), BF16),
            vmem((BANDS, 1, 128), F32),
            vmem((BANDS, 1, 128), F32),
            vmem((LON, 16, WAVES), BF16),
            vmem((LON, 16, WAVES), BF16),
            pltpu.SemaphoreType.DMA((5,)),
            pltpu.SemaphoreType.DMA((5,)),
            pltpu.SemaphoreType.DMA((5,)),
        ],
        compiler_params=pltpu.CompilerParams(
            collective_id=0, has_side_effects=True, vmem_limit_bytes=60 * 1024 * 1024
        ),
    )(latitudes, orders, layers, temperature, moisture, ground, operator, polynomial)
    return flat.reshape(4, 2, 2, WAVES)


def solution(mesh):
    placed = (
        P("band", None, "lon"),
        P("band", None, "lon"),
        P("band", "lon"),
        P(),
        P("band", "lon", None, None),
        P("band"),
        P("band"),
        P(),
    )
    return jax.shard_map(
        body, mesh=mesh, in_specs=placed, out_specs=P("band", None, "lon", None), check_vma=False
    )
```

```python
import jax
import jax.numpy as jnp
from jax import lax
from jax.experimental import pallas as pl
from jax.experimental.pallas import tpu as pltpu
from jax.sharding import PartitionSpec as P

Z, Y, CORES, LON = 12, 8, 2, 4
YC = Y * CORES
BANDS = Z * YC
LEVELS = 8
WAVES = 768
WIDEST = 5136
PIECE = WIDEST // LON
HALF = 768
BLOCK = 256
BLOCKS = LON * 2 * (HALF // BLOCK)
F32, BF16, I32 = jnp.float32, jnp.bfloat16, jnp.int32
MESH = pl.DeviceIdType.MESH

COS = (1.0, -4.93480110168457, 4.058692932128906, -1.335150122642517, 0.2350122481584549, -0.025341978296637535, 0.0015877870609983802)
SIN = (3.1415927410125732, -5.167712688446045, 2.5501599311828613, -0.5992405414581299, 0.08207812905311584, -0.007271677255630493, 0.000393970258301124)


def far_first(count):
    return sorted(range(count), key=lambda o: -min(o, count - o))


def iota(shape, dim):
    return lax.broadcasted_iota(I32, shape, dim)


def circle(product, length, inverse):
    residue = product - jnp.round(product * inverse) * length
    x = residue * (inverse * 2.0)
    y = x * x
    c = COS[-1]
    s = SIN[-1]
    for a, b in zip(COS[-2::-1], SIN[-2::-1]):
        c = c * y + a
        s = s * y + b
    return c, s * x


def row_length(latitude):
    distance = jnp.minimum(latitude, LON * BANDS - 1 - latitude)
    return WIDEST - 4 * (LON * BANDS // 2 - 1 - distance)


def permuted_operator(operator, layers):
    t = iota((LEVELS, 1), 0)
    level = jnp.zeros((LEVELS, 1), I32)
    for i in range(LEVELS):
        level = jnp.where(t == i, layers[i], level)
    out = jnp.zeros((LEVELS, LEVELS), F32)
    for i in range(LEVELS):
        out = jnp.where(level == i, operator[i : i + 1, :], out)
    return out


def vertical_sum(temperature, moisture, ground, operator):
    virtual = temperature.astype(F32) * (1.0 + 0.608 * moisture.astype(F32))
    total = operator[:, 0:1] * virtual[0:1, :]
    for j in range(1, LEVELS):
        total = total + operator[:, j : j + 1] * virtual[j : j + 1, :]
    return total + ground.astype(F32)


def pack_piece(low, high, lon, length):
    both = jnp.concatenate([low, high], axis=0)
    point = lon * PIECE + jnp.where(iota((16, HALF), 0) >= 8, HALF, 0) + iota((16, HALF), 1)
    return jnp.where(point < length, both, 0.0).astype(BF16)


def phase_points():
    a = iota((BLOCKS, 128), 0)
    return ((a >> 3) * BLOCK + ((a >> 1) & 3) * PIECE + (a & 1) * HALF).astype(F32)


def legendre_row_of(row):
    return (row >> 2) & 3


def placement():
    r, column = iota((16, 512), 0), iota((16, 512), 1)
    slot, level = column >> 7, r & 7
    lane = (level >> 1) * 16 + slot * 4 + (r >> 3) * 2 + (level & 1)
    return jnp.where(lane == (column & 127), 1.0, 0.0).astype(BF16)


def dot(a, b):
    return jnp.dot(a, b, preferred_element_type=F32)


def kernel(
    latitudes_at, orders_at, layers_at, temperature, moisture, ground, operator, polynomial,
    out,
    latitudes, orders, layers, t_in, q_in, g_in, o_in, p_in, fields, piece_out, piece_in, order_1, order_2,
    tables, phases, columns, row_out, row_in, part_out, part_in,
    load_sem, send_sem, recv_sem,
):
    band, lon = lax.axis_index("band"), lax.axis_index("lon")
    z, yc = band // YC, band % YC
    y, core = yc // CORES, yc % CORES

    def over_z(o):
        return lax.rem(z + o, Z)

    def over_yc(o):
        return lax.rem(yc + o, YC)

    def over_lon(o):
        return lax.rem(lon + o, LON)

    barrier = pltpu.get_barrier_semaphore()
    for o in far_first(Z)[:-1]:
        pl.semaphore_signal(barrier, 1, device_id={"band": over_z(o) * YC + yc}, device_id_type=MESH)
    for o in far_first(LON)[:-1]:
        pl.semaphore_signal(barrier, 1, device_id={"lon": over_lon(o)}, device_id_type=MESH)
    for o in far_first(YC)[:-1]:
        pl.semaphore_signal(barrier, 1, device_id={"band": z * YC + over_yc(o)}, device_id_type=MESH)

    loads = [
        pltpu.make_async_copy(source, target, load_sem.at[i])
        for i, (source, target) in enumerate(
            (
                (orders_at, orders), (layers_at, layers), (latitudes_at, latitudes),
                (operator, o_in), (temperature, t_in), (moisture, q_in), (ground, g_in), (polynomial.at[:, 0], p_in),
            )
        )
    ]
    for load in loads:
        load.start()

    sent = []

    def exchange(stage, count, partner, source, target, whole):
        sent.append((stage, whole.at[pl.ds(0, count - 1)]))
        for o in far_first(count)[:-1]:
            pltpu.make_async_remote_copy(
                src_ref=source(o), dst_ref=target, send_sem=send_sem.at[stage], recv_sem=recv_sem.at[stage],
                device_id=partner(o), device_id_type=MESH,
            ).start()

    def wait_recv(stage, ref):
        pltpu.make_async_copy(ref, ref, recv_sem.at[stage]).wait()

    def finish():
        for stage, ref in sent:
            pltpu.make_async_copy(ref, ref, send_sem.at[stage]).wait()

    def to_yc(o):
        return {"band": z * YC + over_yc(o)}

    def to_z(o):
        return {"band": over_z(o) * YC + yc}

    def to_lon(o):
        return {"lon": over_lon(o)}

    loads[0].wait()
    lane = iota((1, 128), 1)
    row = jnp.zeros((1, 128), I32)
    for s in range(4):
        digit = jnp.where(lane < 64, orders[s] & ~31, orders[s] & 31)
        row = jnp.where((lane & 63) == yc * 4 + s, digit, row)
    order_1[yc] = row.astype(F32)
    fields[:, :, 1280:] = jnp.zeros((4, LEVELS, 2 * HALF - 1280), F32)
    pl.semaphore_wait(barrier, LON + YC + Z - 3)
    exchange(0, YC, to_yc, lambda o: order_1.at[yc], order_1.at[yc], order_1)

    for load in loads[1:7]:
        load.wait()
    operator_rows = permuted_operator(o_in[...], [layers[i] for i in range(LEVELS)])
    for r in range(4):
        fields[r, :, :PIECE] = vertical_sum(t_in[r], q_in[r], g_in[r : r + 1], operator_rows)
        piece_out[r] = pack_piece(fields[r, :, :HALF], fields[r, :, HALF:], lon, row_length(latitudes[r]))
    exchange(1, LON, to_lon, lambda o: piece_out.at[over_lon(o)], piece_in.at[lon], piece_out)
    piece_in[lon] = piece_out[lon]

    wait_recv(0, order_1.at[pl.ds(0, YC - 1)])
    order_2[z] = jnp.sum(order_1[...], axis=0)
    exchange(2, Z, to_z, lambda o: order_2.at[z], order_2.at[z], order_2)

    length = jnp.full((1, 128), row_length(latitudes[lon]), I32).astype(F32)
    inverse = 1.0 / length

    def table(n, carry):
        m = (n * 128 + iota((1, 128), 1)).astype(F32)
        step = iota((16, 128), 0).astype(F32)
        c0, s0 = circle(step * m, length, inverse)
        c1, s1 = circle(step * 16.0 * m, length, inverse)
        for b in range(16):
            c, s = c1[b : b + 1], s1[b : b + 1]
            tables[n, b * 16 : b * 16 + 16, :128] = (c * c0 - s * s0).astype(BF16)
            tables[n, b * 16 : b * 16 + 16, 128:] = (s * c0 + c * s0).astype(BF16)
        c, s = circle(phase_points() * m, length, inverse)
        phases[n, :, :128] = c * inverse
        phases[n, :, 128:] = s * inverse
        return carry

    lax.fori_loop(0, WAVES // 128, table, 0)

    wait_recv(1, piece_in.at[pl.ds(0, LON - 1)])

    def transform(n, carry):
        c = jnp.zeros((8, 128), F32)
        s = jnp.zeros((8, 128), F32)
        for j in range(HALF // BLOCK):
            block = piece_in[:, :, j * BLOCK : (j + 1) * BLOCK].reshape(LON * 16, BLOCK)
            sums = dot(block, tables[n])
            for i in range(8):
                a = j * 8 + i
                pc, ps = phases[n, a : a + 1, :128], phases[n, a : a + 1, 128:]
                gc, gs = sums[i * 8 : i * 8 + 8, :128], sums[i * 8 : i * 8 + 8, 128:]
                c = c + (pc * gc - ps * gs)
                s = s - (ps * gc + pc * gs)
        turned = jnp.concatenate([c, s], axis=0).T.astype(BF16)
        placed = dot(turned, placement()).astype(BF16)
        for s in range(4):
            columns[s, pl.ds(pl.multiple_of(n * 128, 128), 128), :] = placed[:, s * 128 : (s + 1) * 128]
        return carry

    lax.fori_loop(0, WAVES // 128, transform, 0)

    wait_recv(2, order_2.at[pl.ds(0, Z - 1)])
    own = ((iota((Y, 128), 1) & 63) >> 3) == iota((Y, 128), 0)
    digits = jnp.concatenate([jnp.where(own, order_2[i], 0.0) for i in range(Z)], axis=0).astype(BF16)
    held = dot(digits, jnp.where((iota((128, 128), 0) & 7) == iota((128, 128), 1), 1.0, 0.0).astype(BF16))
    wave = iota((Z * Y, WAVES), 1).astype(F32)
    for c in range(CORES):
        rows = jnp.zeros((Z * Y, 128), F32)
        for s in range(4):
            i = c * 4 + s
            chosen = jnp.where(held[:, i : i + 1] == wave, 1.0, 0.0).astype(BF16)
            rows = rows + dot(chosen, columns[s])
        row_out[c * Z * Y : (c + 1) * Z * Y] = rows.reshape(Z * Y, 1, 128)

    def to_band(target_z, target_y, target_core):
        pltpu.make_async_remote_copy(
            src_ref=row_out.at[target_core * (Z * Y) + target_z * Y + target_y], dst_ref=row_in.at[band],
            send_sem=send_sem.at[3], recv_sem=recv_sem.at[3],
            device_id={"band": (target_z * Y + target_y) * CORES + target_core}, device_id_type=MESH,
        ).start()

    targets = []
    for d in far_first(Y):
        target_y = y + d
        target_y = jnp.where(target_y >= Y, target_y - Y, target_y)
        targets += [(target_y, 1 - core), (target_y, core)]

    def to_other_z(i, carry):
        half = (i + 1) // 2
        target_z = z + Z // 2 + jnp.where(i % 2 == 1, -half, half)
        target_z = jnp.where(target_z >= Z, target_z - Z, target_z)
        for target in targets:
            to_band(target_z, *target)
        return carry

    lax.fori_loop(0, Z - 1, to_other_z, 0)
    for target in targets[:-1]:
        to_band(z, *target)
    sent.append((3, row_out.at[pl.ds(0, BANDS - 1)]))
    row_in[band] = row_out[core * (Z * Y) + z * Y + y]
    loads[7].wait()
    wait_recv(3, row_in.at[pl.ds(0, BANDS - 1)])

    rows = row_in[...].reshape(BANDS, 128).T[:64]
    slot = legendre_row_of(iota((64, BANDS), 0))
    own_slot = [jnp.where(slot == s, rows, 0.0).astype(BF16) for s in range(4)]
    for n in range(WAVES // BLOCK):
        total = dot(own_slot[0], p_in[0, :, n * BLOCK : (n + 1) * BLOCK])
        for s in range(1, 4):
            total = total + dot(own_slot[s], p_in[s, :, n * BLOCK : (n + 1) * BLOCK])
        part_out[n] = total.reshape(LON, 16, BLOCK).astype(BF16)
        part = part_in.at[n]
        exchange(4 + n, LON, to_lon, lambda o: part_out.at[n, over_lon(o)], part.at[lon], part_out.at[n])
        part[lon] = part_out[n, lon]

    slot = legendre_row_of(iota((16, 1), 0))
    limit = jnp.zeros((16, 1), I32)
    for s in range(4):
        limit = jnp.where(slot == s, WAVES - orders[s], limit)
    for n in range(WAVES // BLOCK):
        wait_recv(4 + n, part_in.at[n, pl.ds(0, LON - 1)])
        part = [part_in[n, i].astype(F32) for i in range(LON)]
        summed = (part[0] + part[1]) + (part[2] + part[3])
        out[:, n * BLOCK : (n + 1) * BLOCK] = jnp.where(n * BLOCK + iota((16, BLOCK), 1) < limit, summed, 0.0)

    finish()


def body(temperature, moisture, ground, operator, polynomial, latitudes, orders, layers):
    anywhere = pl.BlockSpec(memory_space=pl.ANY)
    vmem = pltpu.VMEM
    flat = pl.pallas_call(
        kernel,
        out_shape=jax.ShapeDtypeStruct((16, WAVES), F32),
        in_specs=[anywhere] * 8,
        out_specs=pl.BlockSpec(memory_space=pltpu.VMEM),
        scratch_shapes=[
            pltpu.SMEM(latitudes.shape, I32),
            pltpu.SMEM(orders.shape, I32),
            pltpu.SMEM(layers.shape, I32),
            vmem(temperature.shape, BF16),
            vmem(moisture.shape, BF16),
            vmem(ground.shape, BF16),
            vmem(operator.shape, F32),
            vmem((4, BANDS, WAVES), BF16),
            vmem((4, LEVELS, 2 * HALF), F32),
            vmem((LON, 16, HALF), BF16),
            vmem((LON, 16, HALF), BF16),
            vmem((YC, 1, 128), F32),
            vmem((Z, 1, 128), F32),
            vmem((WAVES // 128, BLOCK, 256), BF16),
            vmem((WAVES // 128, BLOCKS, 256), F32),
            vmem((4, WAVES, 128), BF16),
            vmem((BANDS, 1, 128), F32),
            vmem((BANDS, 1, 128), F32),
            vmem((WAVES // BLOCK, LON, 16, BLOCK), BF16),
            vmem((WAVES // BLOCK, LON, 16, BLOCK), BF16),
            pltpu.SemaphoreType.DMA((8,)),
            pltpu.SemaphoreType.DMA((7,)),
            pltpu.SemaphoreType.DMA((7,)),
        ],
        compiler_params=pltpu.CompilerParams(
            collective_id=0, has_side_effects=True, vmem_limit_bytes=60 * 1024 * 1024
        ),
    )(latitudes, orders, layers, temperature, moisture, ground, operator, polynomial)
    return flat.reshape(4, 2, 2, WAVES)


def solution(mesh):
    placed = (
        P("band", None, "lon"),
        P("band", None, "lon"),
        P("band", "lon"),
        P(),
        P("band", "lon", None, None),
        P("band"),
        P("band"),
        P(),
    )
    return jax.shard_map(
        body, mesh=mesh, in_specs=placed, out_specs=P("band", None, "lon", None), check_vma=False
    )
```

```python
import jax
import jax.numpy as jnp
from jax import lax
from jax.experimental import pallas as pl
from jax.experimental.pallas import tpu as pltpu
from jax.sharding import PartitionSpec as P

Z, Y, CORES, LON = 12, 8, 2, 4
YC = Y * CORES
BANDS = Z * YC
LEVELS = 8
WAVES = 768
WIDEST = 5136
PIECE = WIDEST // LON
HALF = 768
BLOCK = 256
BLOCKS = LON * 2 * (HALF // BLOCK)
F32, BF16, I32 = jnp.float32, jnp.bfloat16, jnp.int32
MESH = pl.DeviceIdType.MESH

COS = (1.0, -4.93480110168457, 4.058692932128906, -1.335150122642517, 0.2350122481584549, -0.025341978296637535, 0.0015877870609983802)
SIN = (3.1415927410125732, -5.167712688446045, 2.5501599311828613, -0.5992405414581299, 0.08207812905311584, -0.007271677255630493, 0.000393970258301124)


def far_first(count):
    return sorted(range(count), key=lambda o: -min(o, count - o))


def iota(shape, dim):
    return lax.broadcasted_iota(I32, shape, dim)


def circle(product, length, inverse):
    residue = product - jnp.round(product * inverse) * length
    x = residue * (inverse * 2.0)
    y = x * x
    c = COS[-1]
    s = SIN[-1]
    for a, b in zip(COS[-2::-1], SIN[-2::-1]):
        c = c * y + a
        s = s * y + b
    return c, s * x


def row_length(latitude):
    distance = jnp.minimum(latitude, LON * BANDS - 1 - latitude)
    return WIDEST - 4 * (LON * BANDS // 2 - 1 - distance)


def permuted_operator(operator, layers):
    t = iota((LEVELS, 1), 0)
    level = jnp.zeros((LEVELS, 1), I32)
    for i in range(LEVELS):
        level = jnp.where(t == i, layers[i], level)
    out = jnp.zeros((LEVELS, LEVELS), F32)
    for i in range(LEVELS):
        out = jnp.where(level == i, operator[i : i + 1, :], out)
    return out


def vertical_sum(temperature, moisture, ground, operator):
    virtual = temperature.astype(F32) * (1.0 + 0.608 * moisture.astype(F32))
    total = operator[:, 0:1] * virtual[0:1, :]
    for j in range(1, LEVELS):
        total = total + operator[:, j : j + 1] * virtual[j : j + 1, :]
    return total + ground.astype(F32)


def pack_piece(low, high, lon, length):
    both = jnp.concatenate([low, high], axis=0)
    point = lon * PIECE + jnp.where(iota((16, HALF), 0) >= 8, HALF, 0) + iota((16, HALF), 1)
    return jnp.where(point < length, both, 0.0).astype(BF16)


def phase_points():
    a = iota((BLOCKS, 128), 0)
    return ((a >> 3) * BLOCK + ((a >> 1) & 3) * PIECE + (a & 1) * HALF).astype(F32)


def legendre_row_of(row):
    return (row >> 2) & 3


def placement():
    r, column = iota((16, 512), 0), iota((16, 512), 1)
    slot, level = column >> 7, r & 7
    lane = (level >> 1) * 16 + slot * 4 + (r >> 3) * 2 + (level & 1)
    return jnp.where(lane == (column & 127), 1.0, 0.0).astype(BF16)


def dot(a, b):
    return jnp.dot(a, b, preferred_element_type=F32)


def kernel(
    latitudes_at, orders_at, layers_at, temperature, moisture, ground, operator, polynomial,
    out,
    latitudes, orders, layers, t_in, q_in, g_in, o_in, p_in, fields, piece_out, piece_in, order_1, order_2,
    tables, phases, columns, row_out, row_in, part_out, part_in,
    load_sem, send_sem, recv_sem,
):
    band, lon = lax.axis_index("band"), lax.axis_index("lon")
    z, yc = band // YC, band % YC
    y, core = yc // CORES, yc % CORES

    def over_z(o):
        return lax.rem(z + o, Z)

    def over_yc(o):
        return lax.rem(yc + o, YC)

    def over_lon(o):
        return lax.rem(lon + o, LON)

    barrier = pltpu.get_barrier_semaphore()
    for o in far_first(Z)[:-1]:
        pl.semaphore_signal(barrier, 1, device_id={"band": over_z(o) * YC + yc}, device_id_type=MESH)
    for o in far_first(LON)[:-1]:
        pl.semaphore_signal(barrier, 1, device_id={"lon": over_lon(o)}, device_id_type=MESH)
    for o in far_first(YC)[:-1]:
        pl.semaphore_signal(barrier, 1, device_id={"band": z * YC + over_yc(o)}, device_id_type=MESH)

    loads = [
        pltpu.make_async_copy(source, target, load_sem.at[i])
        for i, (source, target) in enumerate(
            (
                (orders_at, orders), (layers_at, layers), (latitudes_at, latitudes),
                (operator, o_in), (temperature, t_in), (moisture, q_in), (ground, g_in), (polynomial.at[:, 0], p_in),
            )
        )
    ]
    for load in loads:
        load.start()

    sent = []

    def exchange(stage, count, partner, source, target, whole):
        sent.append((stage, whole.at[pl.ds(0, count - 1)]))
        for o in far_first(count)[:-1]:
            pltpu.make_async_remote_copy(
                src_ref=source(o), dst_ref=target, send_sem=send_sem.at[stage], recv_sem=recv_sem.at[stage],
                device_id=partner(o), device_id_type=MESH,
            ).start()

    def wait_recv(stage, ref):
        pltpu.make_async_copy(ref, ref, recv_sem.at[stage]).wait()

    def finish():
        for stage, ref in sent:
            pltpu.make_async_copy(ref, ref, send_sem.at[stage]).wait()

    def to_yc(o):
        return {"band": z * YC + over_yc(o)}

    def to_z(o):
        return {"band": over_z(o) * YC + yc}

    def to_lon(o):
        return {"lon": over_lon(o)}

    loads[0].wait()
    lane = iota((1, 128), 1)
    row = jnp.zeros((1, 128), I32)
    for s in range(4):
        digit = jnp.where(lane < 64, orders[s] & ~31, orders[s] & 31)
        row = jnp.where((lane & 63) == yc * 4 + s, digit, row)
    order_1[yc] = row.astype(F32)
    fields[:, :, 1280:] = jnp.zeros((4, LEVELS, 2 * HALF - 1280), F32)
    pl.semaphore_wait(barrier, LON + YC + Z - 3)
    exchange(0, YC, to_yc, lambda o: order_1.at[yc], order_1.at[yc], order_1)

    for load in loads[1:7]:
        load.wait()
    operator_rows = permuted_operator(o_in[...], [layers[i] for i in range(LEVELS)])
    for r in range(4):
        fields[r, :, :PIECE] = vertical_sum(t_in[r], q_in[r], g_in[r : r + 1], operator_rows)
        piece_out[r] = pack_piece(fields[r, :, :HALF], fields[r, :, HALF:], lon, row_length(latitudes[r]))
    exchange(1, LON, to_lon, lambda o: piece_out.at[over_lon(o)], piece_in.at[lon], piece_out)
    piece_in[lon] = piece_out[lon]

    wait_recv(0, order_1.at[pl.ds(0, YC - 1)])
    order_2[z] = jnp.sum(order_1[...], axis=0)
    exchange(2, Z, to_z, lambda o: order_2.at[z], order_2.at[z], order_2)

    length = jnp.full((1, 128), row_length(latitudes[lon]), I32).astype(F32)
    inverse = 1.0 / length

    def table(n, carry):
        m = (n * 128 + iota((1, 128), 1)).astype(F32)
        step = iota((16, 128), 0).astype(F32)
        c0, s0 = circle(step * m, length, inverse)
        c1, s1 = circle(step * 16.0 * m, length, inverse)
        for b in range(16):
            c, s = c1[b : b + 1], s1[b : b + 1]
            tables[n, b * 16 : b * 16 + 16, :128] = (c * c0 - s * s0).astype(BF16)
            tables[n, b * 16 : b * 16 + 16, 128:] = (s * c0 + c * s0).astype(BF16)
        c, s = circle(phase_points() * m, length, inverse)
        phases[n, :, :128] = c * inverse
        phases[n, :, 128:] = s * inverse
        return carry

    lax.fori_loop(0, WAVES // 128, table, 0)

    wait_recv(1, piece_in.at[pl.ds(0, LON - 1)])

    def transform(n, carry):
        c = jnp.zeros((8, 128), F32)
        s = jnp.zeros((8, 128), F32)
        for j in range(HALF // BLOCK):
            block = piece_in[:, :, j * BLOCK : (j + 1) * BLOCK].reshape(LON * 16, BLOCK)
            sums = dot(block, tables[n])
            for i in range(8):
                a = j * 8 + i
                pc, ps = phases[n, a : a + 1, :128], phases[n, a : a + 1, 128:]
                gc, gs = sums[i * 8 : i * 8 + 8, :128], sums[i * 8 : i * 8 + 8, 128:]
                c = c + (pc * gc - ps * gs)
                s = s - (ps * gc + pc * gs)
        turned = jnp.concatenate([c, s], axis=0).T.astype(BF16)
        placed = dot(turned, placement()).astype(BF16)
        for s in range(4):
            columns[s, pl.ds(pl.multiple_of(n * 128, 128), 128), :] = placed[:, s * 128 : (s + 1) * 128]
        return carry

    lax.fori_loop(0, WAVES // 128, transform, 0)

    wait_recv(2, order_2.at[pl.ds(0, Z - 1)])
    own = ((iota((Y, 128), 1) & 63) >> 3) == iota((Y, 128), 0)
    digits = jnp.concatenate([jnp.where(own, order_2[i], 0.0) for i in range(Z)], axis=0).astype(BF16)
    held = dot(digits, jnp.where((iota((128, 128), 0) & 7) == iota((128, 128), 1), 1.0, 0.0).astype(BF16))
    wave = iota((Z * Y, WAVES), 1).astype(F32)
    for c in range(CORES):
        rows = jnp.zeros((Z * Y, 128), F32)
        for s in range(4):
            i = c * 4 + s
            chosen = jnp.where(held[:, i : i + 1] == wave, 1.0, 0.0).astype(BF16)
            rows = rows + dot(chosen, columns[s])
        row_out[c * Z * Y : (c + 1) * Z * Y] = rows.reshape(Z * Y, 1, 128)

    def to_band(target_z, target_y, target_core):
        pltpu.make_async_remote_copy(
            src_ref=row_out.at[target_core * (Z * Y) + target_z * Y + target_y], dst_ref=row_in.at[band],
            send_sem=send_sem.at[3], recv_sem=recv_sem.at[3],
            device_id={"band": (target_z * Y + target_y) * CORES + target_core}, device_id_type=MESH,
        ).start()

    targets = []
    for d in far_first(Y):
        target_y = y + d
        target_y = jnp.where(target_y >= Y, target_y - Y, target_y)
        targets += [(target_y, 1 - core), (target_y, core)]

    def to_other_z(i, carry):
        half = (i + 1) // 2
        target_z = z + Z // 2 + jnp.where(i % 2 == 1, -half, half)
        target_z = jnp.where(target_z >= Z, target_z - Z, target_z)
        for target in targets:
            to_band(target_z, *target)
        return carry

    lax.fori_loop(0, Z - 1, to_other_z, 0)
    for target in targets[:-1]:
        to_band(z, *target)
    sent.append((3, row_out.at[pl.ds(0, BANDS - 1)]))
    row_in[band] = row_out[core * (Z * Y) + z * Y + y]
    loads[7].wait()
    wait_recv(3, row_in.at[pl.ds(0, BANDS - 1)])

    rows = row_in[...].reshape(BANDS, 128).T[:64]
    slot = legendre_row_of(iota((64, BANDS), 0))
    own_slot = [jnp.where(slot == s, rows, 0.0).astype(BF16) for s in range(4)]
    for n in range(WAVES // BLOCK):
        total = dot(own_slot[0], p_in[0, :, n * BLOCK : (n + 1) * BLOCK])
        for s in range(1, 4):
            total = total + dot(own_slot[s], p_in[s, :, n * BLOCK : (n + 1) * BLOCK])
        part_out[n] = total.reshape(LON, 16, BLOCK).astype(BF16)
        part = part_in.at[n]
        exchange(4 + n, LON, to_lon, lambda o: part_out.at[n, over_lon(o)], part.at[lon], part_out.at[n])
        part[lon] = part_out[n, lon]

    slot = legendre_row_of(iota((16, 1), 0))
    limit = jnp.zeros((16, 1), I32)
    for s in range(4):
        limit = jnp.where(slot == s, WAVES - orders[s], limit)
    for n in range(WAVES // BLOCK):
        wait_recv(4 + n, part_in.at[n, pl.ds(0, LON - 1)])
        part = [part_in[n, i].astype(F32) for i in range(LON)]
        summed = (part[0] + part[1]) + (part[2] + part[3])
        out[:, n * BLOCK : (n + 1) * BLOCK] = jnp.where(n * BLOCK + iota((16, BLOCK), 1) < limit, summed, 0.0)

    finish()


def body(temperature, moisture, ground, operator, polynomial, latitudes, orders, layers):
    anywhere = pl.BlockSpec(memory_space=pl.ANY)
    vmem = pltpu.VMEM
    flat = pl.pallas_call(
        kernel,
        out_shape=jax.ShapeDtypeStruct((16, WAVES), F32),
        in_specs=[anywhere] * 8,
        out_specs=pl.BlockSpec(memory_space=pltpu.VMEM),
        scratch_shapes=[
            pltpu.SMEM(latitudes.shape, I32),
            pltpu.SMEM(orders.shape, I32),
            pltpu.SMEM(layers.shape, I32),
            vmem(temperature.shape, BF16),
            vmem(moisture.shape, BF16),
            vmem(ground.shape, BF16),
            vmem(operator.shape, F32),
            vmem((4, BANDS, WAVES), BF16),
            vmem((4, LEVELS, 2 * HALF), F32),
            vmem((LON, 16, HALF), BF16),
            vmem((LON, 16, HALF), BF16),
            vmem((YC, 1, 128), F32),
            vmem((Z, 1, 128), F32),
            vmem((WAVES // 128, BLOCK, 256), BF16),
            vmem((WAVES // 128, BLOCKS, 256), F32),
            vmem((4, WAVES, 128), BF16),
            vmem((BANDS, 1, 128), F32),
            vmem((BANDS, 1, 128), F32),
            vmem((WAVES // BLOCK, LON, 16, BLOCK), BF16),
            vmem((WAVES // BLOCK, LON, 16, BLOCK), BF16),
            pltpu.SemaphoreType.DMA((8,)),
            pltpu.SemaphoreType.DMA((7,)),
            pltpu.SemaphoreType.DMA((7,)),
        ],
        compiler_params=pltpu.CompilerParams(
            collective_id=0, has_side_effects=True, vmem_limit_bytes=32 * 1024 * 1024
        ),
    )(*[pltpu.with_memory_space_constraint(v, pltpu.HBM) for v in (latitudes, orders, layers, temperature, moisture, ground, operator, polynomial)])
    return flat.reshape(4, 2, 2, WAVES)


def solution(mesh):
    placed = (
        P("band", None, "lon"),
        P("band", None, "lon"),
        P("band", "lon"),
        P(),
        P("band", "lon", None, None),
        P("band"),
        P("band"),
        P(),
    )
    return jax.shard_map(
        body, mesh=mesh, in_specs=placed, out_specs=P("band", None, "lon", None), check_vma=False
    )
```
